256 devices in a mesh: dp: 64 (over y_lo, x, z), tok: 4 (over y_hi, core).
Axes of the slice: x: 4, y: 4 (y_hi: 2, y_lo: 2; y = y_hi * 2 + y_lo), z: 8, core: 2. Of those that a mesh axis runs over, the one named last changes fastest.
Arguments:
- queries: bfloat16 [4096, 32, 128], P('dp'), may hold values from -6 to 6
- documents: bfloat16 [8192, 180, 128], P('dp', 'tok'), may hold values from -6 to 6
- lengths: int32 [8192], replicated, may hold values from 1 to 180
Outputs:
- scores: float32 [4096, 2, 128], P('dp')
The draws below stay inside these ranges and needn't reach their ends.
All inputs are finite; a program needn't handle non-finite values.
Results may differ from the reference program's by a relative error of at most 0.00034.
Values may be sent and summed in bfloat16 or wider, within the bound.
No kernel may reach another device: no remote copies, remote signals or barrier semaphores. Data moves between devices by JAX's collectives and lax.ppermute only.
A program may use at most 64 MiB of HBM per device.

```python
import jax
import jax.numpy as jnp
from jax import lax

E = 128
LQ = 32
LD = 180
Q_DEV = 64
DOC_DEV = 128
STEPS = 2
NQ = 4096
ND = 8192
N_DP = 64


def with_ends(values, stream_key, smallest, high):
    dims = values.shape
    spot = [jax.random.randint(jax.random.fold_in(stream_key, axis), (), 0, dims[axis]) for axis in range(len(dims))]
    values = values.at[tuple(spot)].set(smallest)
    longest = dims.index(max(dims))
    spot[longest] = (spot[longest] + 1) % dims[longest]
    return values.at[tuple(spot)].set(high)


def steps_of(rng, extent, pieces, least, largest):
    def one(axis_at, parts):
        heights = jax.random.uniform(jax.random.fold_in(jax.random.fold_in(rng, 6), axis_at), (parts,), jnp.float32, least / len(pieces), largest / len(pieces))
        return jnp.repeat(jnp.exp(heights), extent[axis_at] // parts).reshape((-1,) + (1,) * (len(extent) - axis_at - 1))

    gain = one(*pieces[0])
    for cut in pieces[1:]:
        gain = gain * one(*cut)
    return gain


def centred(key, dims, spread, most, shards=(), kind=jnp.bfloat16):
    level = steps_of(key, dims, shards, -0.22, 0.18) if shards else 1.0
    drawn = jax.random.normal(key, dims, jnp.float32) * spread * level
    return jnp.minimum(jnp.maximum(drawn, -most), most).astype(kind)


def setup_inputs(seed: int = 0) -> dict:
    key_list = jax.random.split(jax.random.key(seed), 4)
    queries = centred(key_list[0], (NQ, LQ, E), 1.0, 6.0, ((0, 64),))
    documents = centred(key_list[1], (ND, LD, E), 1.0, 6.0, ((0, 64), (1, 4)))
    lengths = with_ends(jax.random.randint(key_list[2], (ND,), 1, LD + 1), jax.random.fold_in(key_list[2], 1), 1, LD).astype(jnp.int32)
    return {"queries": queries, "documents": documents, "lengths": lengths}


negative_fill = -1e+30

def normalize(values):
    wide = values.astype(jnp.float32)
    return (wide * lax.rsqrt(lax.optimization_barrier(jnp.sum(wide * wide, axis=-1, keepdims=True)) + 1e-06)).astype(jnp.bfloat16)

def slot_group(count):
    best_size = 1
    for trial in range(1, 9):
        if count % trial == 0:
            best_size = trial
    return best_size

def token_maxima(shard_q, token_major, limits_all, offset):
    qcount, query_len, embed_width = shard_q.shape
    doc_len, dcount, _ = token_major.shape
    group = slot_group(doc_len)
    flat_q = shard_q.reshape(qcount * query_len, embed_width)
    grouped = token_major.reshape(doc_len // group, group * dcount, embed_width)
    position = (offset + jnp.arange(doc_len, dtype=jnp.int32)).reshape(doc_len // group, group)

    def one_group(running, operands):
        doc_tile, slots = operands
        similar = lax.dot_general(flat_q, doc_tile, (((1,), (1,)), ((), ())), preferred_element_type=jnp.float32)
        similar = similar.reshape(qcount * query_len, group, dcount)
        usable = slots[:, None] < limits_all[None, :]
        similar = jnp.where(usable[None], similar, negative_fill)
        return (jnp.maximum(running, lax.optimization_barrier(jnp.max(similar, axis=1))), None)
    start = jnp.full((qcount * query_len, dcount), negative_fill, jnp.float32)
    maxima, _ = lax.scan(one_group, start, (grouped, position))
    return maxima.reshape(qcount, query_len, dcount)

def reference(queries, documents, lengths):
    normed_q = normalize(queries).reshape(N_DP, Q_DEV, LQ, E)
    normed_d = jnp.transpose(normalize(documents), (1, 0, 2)).reshape(LD, N_DP, DOC_DEV, E)
    length_blocks = lengths.reshape(N_DP, DOC_DEV)

    def per_block(block_id):
        stacked = []
        for step_no in range(STEPS):
            source = (block_id - 1 - step_no + N_DP) % N_DP
            maxima = token_maxima(normed_q[block_id], normed_d[:, source], length_blocks[source], 0)
            stacked.append(lax.optimization_barrier(jnp.sum(maxima, axis=1)))
        return jnp.stack(stacked, axis=1)
    result = lax.map(per_block, jnp.arange(N_DP, dtype=jnp.int32))
    return result.reshape(NQ, STEPS, DOC_DEV)
```

```python
import functools

import jax
import jax.numpy as jnp
from jax import lax
from jax.experimental import pallas as pl
from jax.experimental.pallas import tpu as pltpu
from jax.sharding import PartitionSpec as P

STEPS = 2
NEGATIVE_FILL = -1e30
GROUP = 8
SLOT_BLOCK = 16
COLUMNS = 256
VMEM_LIMIT = 40 * 1024 * 1024


def normalized(values):
    wide = values.astype(jnp.float32)
    return wide * lax.rsqrt(jnp.sum(wide * wide, axis=-1, keepdims=True) + 1e-06)


def arrange_queries(half_refs, core, wide_ref, q_ref):
    per_half, tokens, _ = half_refs[0].shape
    stride = 2 * STEPS * per_half
    for place, half_ref in enumerate(half_refs):
        step_no, other = place // 2, place % 2
        half = core if other == 0 else 1 - core

        def norm_one(i, carry, half_ref=half_ref):
            rows = pl.ds(pl.multiple_of(i * tokens, tokens), tokens)
            wide_ref[rows, :] = normalized(half_ref[i])
            return carry

        lax.fori_loop(0, per_half, norm_one, 0, unroll=8)

        def place_token(k, carry, step_no=step_no, half=half):
            first = k * stride + step_no * 2 * per_half + half * per_half
            rows = wide_ref[pl.ds(k, per_half, stride=tokens), :]
            q_ref[pl.ds(pl.multiple_of(first, per_half), per_half), :] = rows.astype(q_ref.dtype)
            return carry

        lax.fori_loop(0, tokens, place_token, 0, unroll=8)


def score_slab(slab_ref, base, order_ref, lens_ref, lens_wide_ref, q_ref, wide_ref, packed_ref, best_ref):
    docs, slots, _ = slab_ref.shape
    padded = -(-slots // SLOT_BLOCK) * SLOT_BLOCK
    blocks = padded // SLOT_BLOCK
    slot = lax.broadcasted_iota(jnp.int32, (slots, 1), 0)

    def norm_one(p, carry):
        rows = normalized(slab_ref[order_ref[p]])
        first = rows[0:1]
        rows = jnp.where(slot < lens_ref[p] - base, rows, first)
        rows = jnp.concatenate([rows, jnp.broadcast_to(first, (padded - slots, first.shape[1]))], axis=0)
        wide_ref[pl.ds(pl.multiple_of(p * padded, padded), padded), :] = rows
        return carry

    used = jnp.int32(0)
    for p in range(docs):
        used = used + (lens_ref[p] > base).astype(jnp.int32)
    groups = (used + GROUP - 1) // GROUP
    lax.fori_loop(0, groups * (GROUP // 4), lambda i, c: lax.fori_loop(0, 4, lambda k, d: norm_one(i * 4 + k, d), c, unroll=True), 0)

    def one_group(g, carry):
        start = g * GROUP * padded
        longest = lens_ref[g * GROUP] - base
        count = jnp.minimum((longest + SLOT_BLOCK - 1) // SLOT_BLOCK, blocks)

        def pack(i, c):
            for k in range(0, SLOT_BLOCK, 2):
                u = i * SLOT_BLOCK + k
                pair = [wide_ref[pl.ds(start + u + e, GROUP, stride=padded), :] for e in range(2)]
                rows = pl.ds(pl.multiple_of(u * GROUP, 2 * GROUP), 2 * GROUP)
                packed_ref[rows, :] = jnp.concatenate(pair, axis=0).astype(packed_ref.dtype)
            return c

        lax.fori_loop(0, count, pack, 0)
        rows_g = pl.ds(pl.multiple_of(g * GROUP, GROUP), GROUP)
        real = lens_wide_ref[rows_g, :][:, 0:1] > base
        for blocks_now in range(1, blocks + 1):

            @pl.when(count == blocks_now)
            def _():
                height = blocks_now * SLOT_BLOCK
                rows = packed_ref[0 : height * GROUP, :]
                for n in range(0, q_ref.shape[0], COLUMNS):
                    similar = lax.dot_general(
                        rows, q_ref[n : n + COLUMNS, :], (((1,), (1,)), ((), ())), preferred_element_type=jnp.float32
                    )
                    top = jnp.max(similar.reshape(height, GROUP, COLUMNS), axis=0)
                    top = jnp.where(real, top, NEGATIVE_FILL)
                    best_ref[rows_g, n : n + COLUMNS] = jnp.maximum(best_ref[rows_g, n : n + COLUMNS], top)

        return carry

    lax.fori_loop(0, groups, one_group, 0)


def early_kernel(where_ref, order_ref, lens_ref, lens_wide_ref, q0, q1, q2, q3, own_ref, near_ref, q_ref, best_ref, qwide_ref, wide_ref, packed_ref):
    tok = where_ref[0]
    slots = own_ref.shape[1]
    arrange_queries((q0, q1, q2, q3), lax.rem(tok, 2), qwide_ref, q_ref)
    best_ref[...] = jnp.full(best_ref.shape, NEGATIVE_FILL, jnp.float32)
    for k, slab_ref in enumerate((own_ref, near_ref)):
        base = (tok ^ k) * slots
        score_slab(slab_ref, base, order_ref, lens_ref, lens_wide_ref, q_ref, wide_ref, packed_ref, best_ref)


def late_kernel(where_ref, order_ref, lens_ref, lens_wide_ref, q_ref, early_ref, far_ref, far_other_ref, out_ref, best_ref, wide_ref, packed_ref, sums_ref):
    tok = where_ref[0]
    slots = far_ref.shape[1]
    best_ref[...] = early_ref[...]
    for k, slab_ref in ((2, far_ref), (3, far_other_ref)):
        base = (tok ^ k) * slots
        score_slab(slab_ref, base, order_ref, lens_ref, lens_wide_ref, q_ref, wide_ref, packed_ref, best_ref)
    docs, lanes = out_ref.shape
    total = best_ref[:, 0:lanes]
    for k in range(lanes, best_ref.shape[1], lanes):
        total = total + best_ref[:, k : k + lanes]
    sums_ref[...] = total

    def unsort(p, carry):
        out_ref[pl.ds(order_ref[p], 1), :] = sums_ref[pl.ds(p, 1), :]
        return carry

    lax.fori_loop(0, docs, unsort, 0, unroll=8)


SMEM = pl.BlockSpec(memory_space=pltpu.SMEM)
VMEM = pl.BlockSpec(memory_space=pltpu.VMEM)


def shifted(block, axis, distance):
    size = lax.axis_size(axis)
    return lax.ppermute(block, axis, [(i, (i + distance) % size) for i in range(size)])


def swapped(block, mask):
    return lax.ppermute(block, "tok", [(i, i ^ mask) for i in range(lax.axis_size("tok"))])


def per_device(queries, documents, lengths):
    qcount, tokens, width = queries.shape
    dcount, slots, _ = documents.shape
    tok_size = lax.axis_size("tok")
    tok, dp = lax.axis_index("tok"), lax.axis_index("dp")
    mine = dcount // tok_size
    q_rows = STEPS * qcount * tokens
    lanes = STEPS * qcount
    padded = -(-slots // SLOT_BLOCK) * SLOT_BLOCK

    half = lax.dynamic_slice_in_dim(queries, tok % 2 * (qcount // 2), qcount // 2, 0)
    slabs = [lax.dynamic_slice_in_dim(documents, (tok ^ k) * mine, mine, 0) for k in range(tok_size)]
    arrived = [shifted(half, "dp", -1 - s) for s in range(STEPS)]
    far = [swapped(slabs[k], k) for k in (2, 3)]
    near = swapped(slabs[1], 1)
    halves = []
    for block in arrived:
        halves += [block, swapped(block, 1)]

    lens = lax.dynamic_slice_in_dim(lengths, dp * dcount + tok * mine, mine, 0)
    index = jnp.arange(mine, dtype=jnp.int32)
    ahead = (lens[None, :] > lens[:, None]) | ((lens[None, :] == lens[:, None]) & (index[None, :] < index[:, None]))
    rank = jnp.sum(ahead.astype(jnp.int32), axis=1)
    at = rank[None, :] == index[:, None]
    order = jnp.sum(jnp.where(at, index[None, :], 0), axis=1)
    lens_sorted = jnp.sum(jnp.where(at, lens[None, :], 0), axis=1)
    lens_wide = jnp.broadcast_to(lens_sorted[:, None], (mine, 128))
    where = tok[None].astype(jnp.int32)

    slab_scratch = [
        pltpu.VMEM((mine * padded, width), jnp.float32),
        pltpu.VMEM((GROUP * padded, width), jnp.bfloat16),
    ]
    work = 2 * q_rows * mine * slots * width * 2
    params = pltpu.CompilerParams(vmem_limit_bytes=VMEM_LIMIT)
    q_all, early = pl.pallas_call(
        early_kernel,
        out_shape=(
            jax.ShapeDtypeStruct((q_rows, width), jnp.bfloat16),
            jax.ShapeDtypeStruct((mine, q_rows), jnp.float32),
        ),
        in_specs=[SMEM] * 3 + [VMEM] * 7,
        out_specs=(VMEM, VMEM),
        scratch_shapes=[pltpu.VMEM((qcount // 2 * tokens, width), jnp.float32)] + slab_scratch,
        compiler_params=params,
        cost_estimate=pl.CostEstimate(flops=work, bytes_accessed=1 << 22, transcendentals=0),
        name="early",
    )(where, order, lens_sorted, lens_wide, *halves, slabs[0], near)
    scores = pl.pallas_call(
        late_kernel,
        out_shape=jax.ShapeDtypeStruct((mine, lanes), jnp.float32),
        in_specs=[SMEM] * 3 + [VMEM] * 5,
        out_specs=VMEM,
        scratch_shapes=[pltpu.VMEM((mine, q_rows), jnp.float32)] + slab_scratch + [pltpu.VMEM((mine, lanes), jnp.float32)],
        compiler_params=params,
        cost_estimate=pl.CostEstimate(flops=work, bytes_accessed=1 << 22, transcendentals=0),
        name="late",
    )(where, order, lens_sorted, lens_wide, q_all, early, *far)

    every = lax.all_gather(scores, "tok", axis=0, tiled=True)
    results = [shifted(every[:, s * qcount : (s + 1) * qcount], "dp", 1 + s) for s in range(STEPS)]
    return jnp.stack([block.T for block in results], axis=1)


def solution(mesh):
    in_specs = (P("dp", None, None), P("dp", "tok", None), P())
    out_specs = P("dp", None, None)
    return jax.shard_map(per_device, mesh=mesh, in_specs=in_specs, out_specs=out_specs, check_vma=False)
```

```python
import functools

import jax
import jax.numpy as jnp
from jax import lax
from jax.experimental import pallas as pl
from jax.experimental.pallas import tpu as pltpu
from jax.sharding import PartitionSpec as P

STEPS = 2
NEGATIVE_FILL = -1e30
CHUNK = 16
GROUP = 8
BLOCK = CHUNK * GROUP
NARROW_GROUPS = 4
BATCH = 8
COLUMNS = 256
LANES = 128
VMEM_LIMIT = 40 * 1024 * 1024
SMEM = pl.BlockSpec(memory_space=pltpu.SMEM)
VMEM = pl.BlockSpec(memory_space=pltpu.VMEM)


def normalized(values):
    wide = values.astype(jnp.float32)
    return wide * lax.rsqrt(jnp.sum(wide * wide, axis=-1, keepdims=True) + 1e-06)


def chunks_of(slots):
    return -(-slots // CHUNK)


def prepare_kernel(half_ref, out_ref, wide_ref):
    count, tokens, _ = half_ref.shape

    def norm_one(i, carry):
        rows = pl.ds(pl.multiple_of(i * tokens, tokens), tokens)
        wide_ref[rows, :] = normalized(half_ref[i])
        return carry

    lax.fori_loop(0, count, norm_one, 0, unroll=16)

    def place_token(k, carry):
        out_ref[k] = wide_ref[pl.ds(k, count, stride=tokens), :].astype(out_ref.dtype)
        return carry

    lax.fori_loop(0, tokens, place_token, 0, unroll=16)


def pack(slab_ref, which, offset, info_ref, starts_ref, lens_ref, wide_ref, rows_ref):
    slots, docs, _ = slab_ref.shape
    chunks = chunks_of(slots)
    base = (info_ref[0] ^ which) * slots
    first = normalized(slab_ref[0])
    wide_ref[0:docs, :] = first
    for u in range(slots, chunks * CHUNK):
        wide_ref[u * docs : (u + 1) * docs, :] = first

    def norm_one(u, carry):
        rows = pl.ds(pl.multiple_of(u * docs, docs), docs)
        wide_ref[rows, :] = jnp.where(u + base < lens_ref[...], normalized(slab_ref[u]), first)
        return carry

    lax.fori_loop(1, slots, norm_one, 0, unroll=True)

    def place_one(j, carry):
        start = starts_ref[which * docs + j] - offset
        for c in range(chunks):
            at = start + c
            group = at // GROUP
            rows = wide_ref[pl.ds(c * CHUNK * docs + j, CHUNK, stride=docs), :]
            rows_ref[pl.ds(group * BLOCK + at - group * GROUP, CHUNK, stride=GROUP), :] = rows
        return carry

    lax.fori_loop(0, docs, place_one, 0, unroll=16)


def narrow(rows_ref, packed_ref, count, shift=0):
    size = NARROW_GROUPS * BLOCK

    def one(s, carry):
        source = pl.ds(pl.multiple_of(s * size, size), size)
        target = pl.ds(pl.multiple_of(s * size + shift * BLOCK, BLOCK), size)
        packed_ref[target, :] = rows_ref[source, :].astype(packed_ref.dtype)
        return carry

    lax.fori_loop(0, (count + NARROW_GROUPS - 1) // NARROW_GROUPS, one, 0)


def multiply(packed_ref, first, count, q_refs, top_ref):
    tokens, queries, width = q_refs[0].shape
    tiles = len(q_refs) * tokens * queries // LANES
    step = COLUMNS // queries

    def run(s, groups):
        rows = packed_ref[pl.ds(pl.multiple_of(s * BLOCK, BLOCK), groups * BLOCK), :]
        tile = 0
        for q_ref in q_refs:
            for k in range(0, tokens, step):
                q = q_ref[k : k + step].reshape(COLUMNS, width)
                similar = lax.dot_general(rows, q, (((1,), (1,)), ((), ())), preferred_element_type=jnp.float32)
                top = jnp.max(similar.reshape(groups, CHUNK, GROUP, COLUMNS), axis=1)
                for e in range(0, COLUMNS, LANES):
                    for b in range(groups):
                        place = pl.ds((s + b) * GROUP * tiles + tile, GROUP, stride=tiles)
                        top_ref[place, :] = top[b, :, e : e + LANES]
                    tile += 1

    whole = count // BATCH

    def batch(i, carry):
        run(first + i * BATCH, BATCH)
        return carry

    lax.fori_loop(0, whole, batch, 0)
    size = BATCH // 2
    while size:
        done = count // (2 * size) * (2 * size)

        @pl.when(count - done >= size)
        def _(size=size, done=done):
            run(first + done, size)

        size //= 2


def combine(top_ref, lists, offset, starts_ref, counts_ref, old_ref, best_ref, chunks):
    docs = starts_ref.shape[0] // 4
    tiles = best_ref.shape[0] // docs

    def one(j, carry):
        rows = pl.ds(pl.multiple_of(j * tiles, tiles), tiles)
        best = jnp.full((tiles, LANES), NEGATIVE_FILL, jnp.float32) if old_ref is None else old_ref[rows, :]
        for which in lists:
            start = starts_ref[which * docs + j] - offset
            count = counts_ref[which * docs + j]
            for c in range(chunks):
                top = top_ref[pl.ds(pl.multiple_of((start + c) * tiles, tiles), tiles), :]
                best = jnp.maximum(best, jnp.where(c < count, top, NEGATIVE_FILL))
        best_ref[rows, :] = best
        return carry

    lax.fori_loop(0, docs, one, 0, unroll=16)


def pack_kernel(info, starts, lens, own, near, packed_ref, wide_ref, rows_ref):
    pack(own, 0, 0, info, starts, lens, wide_ref, rows_ref)
    pack(near, 1, 0, info, starts, lens, wide_ref, rows_ref)
    narrow(rows_ref, packed_ref, info[3])


def early_kernel(info, starts, counts, packed, qa, qb, best_ref, top_ref, *, chunks):
    multiply(packed, 0, info[3], (qa, qb), top_ref)
    combine(top_ref, (0, 1), 0, starts, counts, None, best_ref, chunks)


def middle_kernel(info, starts, counts, lens, far, qa, qb, old, packed_ref, best_ref, wide_ref, rows_ref, top_ref):
    offset = info[3] * GROUP
    pack(far, 2, offset, info, starts, lens, wide_ref, rows_ref)
    groups = info[4] - info[3]
    narrow(rows_ref, packed_ref, groups)
    multiply(packed_ref, 0, groups, (qa, qb), top_ref)
    combine(top_ref, (2,), offset, starts, counts, old, best_ref, chunks_of(far.shape[0]))


def token_sums(best_ref, first, docs, tiles, per_half, count):
    total = best_ref[pl.ds(first, docs, stride=tiles), :]
    for k in range(first + 1, first + per_half):
        total = total + best_ref[pl.ds(k, docs, stride=tiles), :]
    shift = LANES // 2
    while shift >= count:
        total = total + pltpu.roll(total, shift, 1)
        shift //= 2
    return total


def query_sums(best_ref, step_no, tok, docs, count):
    tiles = best_ref.shape[0] // docs
    half = lax.rem(tok, 2)
    lane_group = lax.broadcasted_iota(jnp.int32, (docs, LANES), 1) // count
    merged = jnp.zeros((docs, LANES), jnp.float32)
    for other in range(2):
        part = token_sums(best_ref, other * (tiles // 2), docs, tiles, tiles // 2, count)
        place = 2 * step_no + (half if other == 0 else 1 - half)
        merged = jnp.where(lane_group == place, part, merged)
    return merged


def last_slab_kernel(
    info, starts, counts, lens, far, near_packed, far_packed, qa, qb, old, packed_ref, sums_ref,
    best_ref, wide_ref, rows_ref, top_ref,
):
    slots, docs, _ = far.shape
    narrow(near_packed, packed_ref, info[3])
    narrow(far_packed, packed_ref, info[4] - info[3], info[3])
    pack(far, 3, info[4] * GROUP, info, starts, lens, wide_ref, rows_ref)
    narrow(rows_ref, packed_ref, info[5] - info[4], info[4])
    multiply(packed_ref, info[4], info[5] - info[4], (qa, qb), top_ref)
    combine(top_ref, (3,), 0, starts, counts, old, best_ref, chunks_of(slots))
    sums_ref[...] = query_sums(best_ref, 0, info[0], docs, qa.shape[1])


def late_kernel(info, starts, counts, packed, qa, qb, sums, out_ref, best_ref, top_ref, *, chunks):
    docs = sums.shape[0]
    multiply(packed, 0, info[5], (qa, qb), top_ref)
    combine(top_ref, (0, 1, 2, 3), 0, starts, counts, None, best_ref, chunks)
    out_ref[...] = sums[...] + query_sums(best_ref, 1, info[0], docs, qa.shape[1])


def shifted(block, axis, distance):
    size = lax.axis_size(axis)
    return lax.ppermute(block, axis, [(i, (i + distance) % size) for i in range(size)])


def swapped(block, mask):
    return lax.ppermute(block, "tok", [(i, i ^ mask) for i in range(lax.axis_size("tok"))])


def returned(block, mask):
    dp_size, tok_size = lax.axis_size("dp"), lax.axis_size("tok")
    route = [
        (i * tok_size + t, (i + 1 + t % 2) % dp_size * tok_size + (t ^ mask))
        for i in range(dp_size)
        for t in range(tok_size)
    ]
    return lax.ppermute(block, ("dp", "tok"), route)


def in_order(own, other, own_first):
    return jnp.where(own_first, jnp.concatenate([own, other], axis=0), jnp.concatenate([other, own], axis=0))


def per_device(queries, documents, lengths):
    qcount, tokens, width = queries.shape
    dcount, slots, _ = documents.shape
    tok_size = lax.axis_size("tok")
    tok, dp = lax.axis_index("tok"), lax.axis_index("dp")
    core = tok % 2
    mine = dcount // tok_size
    half = qcount // 2
    tiles = qcount * tokens // LANES
    chunks = chunks_of(slots)
    list_rows = mine * chunks * CHUNK
    spare = NARROW_GROUPS * BLOCK
    params = pltpu.CompilerParams(vmem_limit_bytes=VMEM_LIMIT)
    cost = pl.CostEstimate(flops=1 << 10, bytes_accessed=1 << 10, transcendentals=0)
    bf16, f32 = jnp.bfloat16, jnp.float32

    by_slot = jnp.transpose(documents, (1, 0, 2))
    slabs = [lax.dynamic_slice_in_dim(by_slot, (tok ^ k) * mine, mine, 1) for k in range(tok_size)]
    prepared = pl.pallas_call(
        prepare_kernel,
        out_shape=jax.ShapeDtypeStruct((tokens, half, width), bf16),
        in_specs=[VMEM],
        out_specs=VMEM,
        scratch_shapes=[pltpu.VMEM((half * tokens, width), f32)],
        compiler_params=params,
        cost_estimate=cost,
        name="prepare",
    )(lax.dynamic_slice_in_dim(queries, core * half, half, 0))
    arrived = shifted(prepared, "dp", -1)
    far = swapped(slabs[2], 2)
    far_other = swapped(slabs[3], 3)
    near = swapped(slabs[1], 1)

    lens = lax.dynamic_slice_in_dim(lengths, dp * dcount + tok * mine, mine, 0)
    bases = (tok ^ jnp.arange(tok_size, dtype=jnp.int32)) * slots
    counts = jnp.clip((lens[None, :] - bases[:, None] + CHUNK - 1) // CHUNK, 0, chunks)
    index = jnp.arange(mine)
    before = jnp.sum(jnp.where(index[None, None, :] < index[None, :, None], counts[:, None, :], 0), axis=2)
    groups = (jnp.sum(counts, axis=1) + GROUP - 1) // GROUP
    which = jnp.arange(tok_size + 1)
    ends = jnp.sum(jnp.where(which[None, :tok_size] < which[:, None], groups[None, :], 0), axis=1)
    starts = before + ends[:tok_size, None] * GROUP
    info = jnp.concatenate([tok[None], ends]).astype(jnp.int32)
    wide_lens = jnp.broadcast_to(lens[:, None], (mine, LANES))
    starts, counts = starts.reshape(-1), counts.reshape(-1)

    def scratch(lists):
        return [
            pltpu.VMEM((mine * chunks * CHUNK, width), f32),
            pltpu.VMEM((lists * list_rows + spare, width), f32),
        ]

    def tops(lists):
        return pltpu.VMEM((lists * mine * chunks * tiles + 2 * GROUP * tiles, LANES), f32)

    best_shape = jax.ShapeDtypeStruct((mine * tiles, LANES), f32)
    best_scratch = pltpu.VMEM((mine * tiles, LANES), f32)

    def call(kernel, name, out_shape, scratch_shapes, *operands):
        scalar_count = 3 if kernel is not pack_kernel else 2
        return pl.pallas_call(
            kernel,
            out_shape=out_shape,
            in_specs=[SMEM] * scalar_count + [VMEM] * (len(operands) - scalar_count),
            out_specs=jax.tree.map(lambda _: VMEM, out_shape),
            scratch_shapes=scratch_shapes,
            compiler_params=params,
            cost_estimate=cost,
            name=name,
        )(*operands)

    near_packed = call(
        pack_kernel, "pack_near", jax.ShapeDtypeStruct((2 * list_rows + spare, width), bf16), scratch(2),
        info, starts, wide_lens, slabs[0], near,
    )
    arrived, near_packed = lax.optimization_barrier((arrived, near_packed))
    relayed = shifted(arrived, "dp", -1)
    pair = (arrived, swapped(arrived, 1))
    best = call(
        functools.partial(early_kernel, chunks=chunks), "early", best_shape, [tops(2)],
        info, starts, counts, near_packed, *pair,
    )
    far_packed, best = call(
        middle_kernel, "middle", (jax.ShapeDtypeStruct((list_rows + spare, width), bf16), best_shape), scratch(1) + [tops(1)],
        info, starts, counts, wide_lens, far, *pair, best,
    )
    relayed, best = lax.optimization_barrier((relayed, best))
    packed, sums = call(
        last_slab_kernel,
        "last_slab",
        (jax.ShapeDtypeStruct((4 * list_rows + spare, width), bf16), jax.ShapeDtypeStruct((mine, LANES), f32)),
        [best_scratch] + scratch(1) + [tops(4)],
        info, starts, counts, wide_lens, far_other, near_packed, far_packed, *pair, best,
    )
    scores = call(
        functools.partial(late_kernel, chunks=chunks), "late", jax.ShapeDtypeStruct((mine, LANES), f32),
        [best_scratch, tops(4)],
        info, starts, counts, packed, relayed, swapped(relayed, 1), sums,
    )

    chip = in_order(scores, swapped(scores, 1), core == 0)
    sent = jnp.where(core == 0, chip[:, :qcount], chip[:, qcount:])
    block = in_order(returned(sent, 0), returned(sent, 2), tok < 2)
    both = in_order(block[None], swapped(block, 1)[None], core == 0)
    return jnp.transpose(both, (2, 0, 1))


def solution(mesh):
    in_specs = (P("dp", None, None), P("dp", "tok", None), P())
    out_specs = P("dp", None, None)
    return jax.shard_map(per_device, mesh=mesh, in_specs=in_specs, out_specs=out_specs, check_vma=False)
```

```python
import functools

import jax
import jax.numpy as jnp
from jax import lax
from jax.experimental import pallas as pl
from jax.experimental.pallas import tpu as pltpu
from jax.sharding import PartitionSpec as P

STEPS = 2
NEGATIVE_FILL = -1e30
CHUNK = 16
GROUP = 8
BLOCK = CHUNK * GROUP
BATCH = 8
COLUMNS = 256
LANES = 128
RUN = 8
FAR = (3, 2)
SLABS = (0, 1) + FAR
VMEM_LIMIT = 40 * 1024 * 1024
CUT_VMEM_LIMIT = 62 * 1024 * 1024
SMEM = pl.BlockSpec(memory_space=pltpu.SMEM)
VMEM = pl.BlockSpec(memory_space=pltpu.VMEM)
HBM = pl.BlockSpec(memory_space=pltpu.HBM)


def normalized(values):
    wide = values.astype(jnp.float32)
    return wide * lax.rsqrt(jnp.sum(wide * wide, axis=-1, keepdims=True) + 1e-06)


def prepare_kernel(half_ref, out_ref, wide_ref):
    count, tokens, _ = half_ref.shape

    def norm_one(i, carry):
        rows = pl.ds(pl.multiple_of(i * tokens, tokens), tokens)
        wide_ref[rows, :] = normalized(half_ref[i])
        return carry

    lax.fori_loop(0, count, norm_one, 0, unroll=16)

    def place_token(k, carry):
        out_ref[k] = wide_ref[pl.ds(k, count, stride=tokens), :].astype(out_ref.dtype)
        return carry

    lax.fori_loop(0, tokens, place_token, 0, unroll=16)


def cut_kernel(docs_ref, after_ref, *refs):
    del after_ref
    *slab_refs, sems = refs
    mine = slab_refs[0].shape[1]
    cuts = []
    for n in (2, 3, 1, 0):
        first = pl.multiple_of((lax.axis_index("tok") ^ SLABS[n]) * mine, mine)
        cuts.append(pltpu.make_async_copy(docs_ref.at[:, pl.ds(first, mine), :], slab_refs[n], sems.at[n]))
        cuts[-1].start()
    for cut in cuts:
        cut.wait()


def pack(slab_ref, base, starts, first_entry, offset, sort_ref, tall_ref, packed_ref):
    slots, docs, width = slab_ref.shape
    groups = docs // GROUP
    step = sort_ref.shape[0] // docs
    first = normalized(slab_ref[0])
    firsts = jnp.concatenate([first] * step, axis=0)
    slot = lax.broadcasted_iota(jnp.int32, (step * docs, 1), 0) // docs + base
    for u in range(0, -(-slots // CHUNK) * CHUNK, step):
        inside = min(slots - u, step)
        rows = normalized(slab_ref[u : u + inside]).reshape(inside * docs, width)
        if inside < step:
            rows = jnp.concatenate([rows] + [first] * (step - inside), axis=0)
        rows = jnp.where(slot + u < tall_ref[...], rows, firsts).astype(packed_ref.dtype)
        rows = jnp.dot(sort_ref[...], rows, preferred_element_type=jnp.float32)
        start = (starts[first_entry + u // CHUNK] - offset) * BLOCK
        for g in range(groups):
            for v in range(0, step, 2):
                both = [rows[(v + e) * docs + g * GROUP : (v + e) * docs + (g + 1) * GROUP] for e in range(2)]
                at = pl.multiple_of(start + (g * BLOCK + (u % CHUNK + v) * GROUP), 2 * GROUP)
                packed_ref[pl.ds(at, 2 * GROUP), :] = jnp.concatenate(both, axis=0).astype(packed_ref.dtype)


def multiply(packed_ref, count, q_refs, top_ref, batch_blocks=BATCH):
    tokens, queries, width = q_refs[0].shape
    step = COLUMNS // queries

    def run(s, blocks):
        rows = packed_ref[pl.ds(pl.multiple_of(s * BLOCK, BLOCK), blocks * BLOCK), :]
        at = 0
        for q_ref in q_refs:
            for k in range(0, tokens, step):
                q = q_ref[k : k + step].reshape(COLUMNS, width)
                similar = lax.dot_general(rows, q, (((1,), (1,)), ((), ())), preferred_element_type=jnp.float32)
                top = jnp.max(similar.reshape(blocks, CHUNK, GROUP, COLUMNS), axis=1)
                place = pl.ds(pl.multiple_of(s * GROUP, GROUP), blocks * GROUP)
                top_ref[place, at : at + COLUMNS] = top.reshape(blocks * GROUP, COLUMNS)
                at += COLUMNS

    def batch(i, carry):
        run(i * batch_blocks, batch_blocks)
        return carry

    lax.fori_loop(0, count // batch_blocks, batch, 0)
    size = batch_blocks // 2
    while size:
        done = count // (2 * size) * (2 * size)

        @pl.when(count - done >= size)
        def _(size=size, done=done):
            run(done, size)

        size //= 2


def combine(top_ref, lists, offset, starts, lens_ref, old_ref, best_ref, slots, first=0):
    docs, columns = best_ref.shape
    chunks = (starts.shape[0] - 1) // 4
    for g in range(docs // GROUP):
        rows = slice(g * GROUP, (g + 1) * GROUP)
        lens = lens_ref[rows, 0:1]
        best = jnp.full((GROUP, columns), NEGATIVE_FILL, jnp.float32) if old_ref is None else old_ref[rows, :]
        for which in lists:
            for c in range(chunks):
                at = pl.multiple_of((starts[which * chunks + c] - offset + g) * GROUP, GROUP)
                top = top_ref[pl.ds(at, GROUP), first : first + columns]
                real = lens > (lax.axis_index("tok") ^ SLABS[which]) * slots + c * CHUNK
                best = jnp.maximum(best, jnp.where(real, top, NEGATIVE_FILL))
        best_ref[rows, :] = best


def pack_kernel(starts, sort, tall, own, near, packed_ref, *, slots, chunks):
    tok = lax.axis_index("tok")
    for k, slab in enumerate((own, near)):
        pack(slab, (tok ^ k) * slots, starts, k * chunks, 0, sort, tall, packed_ref)


def early_kernel(starts, lens, packed, qa, qb, best_ref, top_ref, *, slots, chunks):
    multiply(packed, starts[2 * chunks], (qa, qb), top_ref)
    combine(top_ref, (0, 1), 0, starts, lens, None, best_ref, slots)


def middle_kernel(starts, lens, sort, tall, far, qa, qb, old, packed_ref, best_ref, top_ref, *, slots, chunks):
    offset = starts[2 * chunks]
    pack(far, (lax.axis_index("tok") ^ FAR[0]) * slots, starts, 2 * chunks, offset, sort, tall, packed_ref)
    multiply(packed_ref, starts[3 * chunks] - offset, (qa, qb), top_ref)
    combine(top_ref, (2,), offset, starts, lens, old, best_ref, slots)


def second_kernel(starts, lens, near_packed, far_packed, qa, qb, best_ref, near_top, far_top, *, slots, chunks):
    offset = starts[2 * chunks]
    multiply(near_packed, offset, (qa, qb), near_top)
    multiply(far_packed, starts[3 * chunks] - offset, (qa, qb), far_top)
    combine(near_top, (0, 1), 0, starts, lens, None, best_ref, slots)
    combine(far_top, (2,), offset, starts, lens, best_ref, best_ref, slots)


def query_sums(best_ref, step_no, tok, count):
    docs, columns = best_ref.shape
    half = lax.rem(tok, 2)
    lane_group = lax.broadcasted_iota(jnp.int32, (docs, LANES), 1) // count
    merged = jnp.zeros((docs, LANES), jnp.float32)
    for other in range(2):
        at = other * columns // 2
        total = best_ref[:, at : at + LANES]
        for k in range(at + LANES, at + columns // 2, LANES):
            total = total + best_ref[:, k : k + LANES]
        shift = LANES // 2
        while shift >= count:
            total = total + pltpu.roll(total, shift, 1)
            shift //= 2
        place = 2 * step_no + (half if other == 0 else 1 - half)
        merged = jnp.where(lane_group == place, total, merged)
    return merged


def late_kernel(
    starts, order, lens, sort, tall, far, q1a, q1b, q2a, q2b, old1, old2, out_ref,
    best_ref, packed_ref, top_ref, sums_ref, *, slots, chunks,
):
    tok = lax.axis_index("tok")
    offset = starts[3 * chunks]
    pack(far, (tok ^ FAR[1]) * slots, starts, 3 * chunks, offset, sort, tall, packed_ref)
    multiply(packed_ref, starts[4 * chunks] - offset, (q1a, q1b, q2a, q2b), top_ref, BATCH // 2)
    docs, columns = best_ref.shape
    total = jnp.zeros((docs, LANES), jnp.float32)
    for s, old in enumerate((old1, old2)):
        combine(top_ref, (3,), offset, starts, lens, old, best_ref, slots, s * columns)
        total = total + query_sums(best_ref, s, tok, q1a.shape[1])
    sums_ref[...] = total

    def unsort(p, carry):
        out_ref[pl.ds(order[p], 1), :] = sums_ref[pl.ds(p, 1), :]
        return carry

    lax.fori_loop(0, docs, unsort, 0, unroll=8)


def wraps(dp, shift):
    return dp % RUN < shift


def handed_back(block, shift, chosen=lambda dp: True):
    dp_size, tok_size = lax.axis_size("dp"), lax.axis_size("tok")
    route = []
    for i in filter(chosen, range(dp_size)):
        for t in range(tok_size):
            mask = 2 if t % 2 and i % (dp_size // 2) < shift else 0
            route.append((i * tok_size + t, (i - shift) % dp_size * tok_size + (t ^ mask)))
    return lax.ppermute(block, ("dp", "tok"), route)


def swapped(block, mask):
    return lax.ppermute(block, "tok", [(i, i ^ mask) for i in range(lax.axis_size("tok"))])


def returned(block, mask):
    dp_size, tok_size = lax.axis_size("dp"), lax.axis_size("tok")
    route = [
        (i * tok_size + t, (i + 1 + t % 2) % dp_size * tok_size + (t ^ mask))
        for i in range(dp_size)
        for t in range(tok_size)
    ]
    return lax.ppermute(block, ("dp", "tok"), route)


def in_order(own, other, own_first):
    return jnp.where(own_first, jnp.concatenate([own, other], axis=0), jnp.concatenate([other, own], axis=0))


def per_device(queries, documents, lengths):
    qcount, tokens, width = queries.shape
    dcount, slots, _ = documents.shape
    tok_size = lax.axis_size("tok")
    tok, dp = lax.axis_index("tok"), lax.axis_index("dp")
    core = tok % 2
    mine = dcount // tok_size
    half = qcount // 2
    columns = qcount * tokens
    chunks = -(-slots // CHUNK)
    groups = mine // GROUP
    params = pltpu.CompilerParams(vmem_limit_bytes=VMEM_LIMIT)
    cost = pl.CostEstimate(flops=1 << 10, bytes_accessed=1 << 10, transcendentals=0)
    bf16, f32 = jnp.bfloat16, jnp.float32

    def call(kernel, name, out_shape, scratch_shapes, scalars, *operands):
        return pl.pallas_call(
            kernel,
            out_shape=out_shape,
            in_specs=[SMEM] * len(scalars) + [VMEM] * len(operands),
            out_specs=jax.tree.map(lambda _: VMEM, out_shape),
            scratch_shapes=scratch_shapes,
            compiler_params=params,
            cost_estimate=cost,
            name=name,
        )(*scalars, *operands)

    prepared = call(
        prepare_kernel, "prepare", jax.ShapeDtypeStruct((tokens, half, width), bf16),
        [pltpu.VMEM((half * tokens, width), f32)], (), lax.dynamic_slice_in_dim(queries, core * half, half, 0),
    )
    arrived = handed_back(prepared, 1)
    slabs = pl.pallas_call(
        cut_kernel,
        out_shape=(jax.ShapeDtypeStruct((slots, mine, width), bf16),) * tok_size,
        in_specs=[HBM, HBM],
        out_specs=(VMEM,) * tok_size,
        scratch_shapes=[pltpu.SemaphoreType.DMA((tok_size,))],
        compiler_params=pltpu.CompilerParams(vmem_limit_bytes=CUT_VMEM_LIMIT),
        cost_estimate=cost,
        name="cut",
    )(jnp.transpose(documents, (1, 0, 2)), prepared)
    own, prepared = lax.optimization_barrier((slabs[0], prepared))
    relayed = handed_back(arrived, 1, lambda i: not wraps(i + 1, 2)) + handed_back(prepared, 2, lambda i: wraps(i, 2))
    near, *fars = [swapped(slabs[n], SLABS[n]) for n in (1, 2, 3)]

    lens = lax.dynamic_slice_in_dim(lengths, dp * dcount + tok * mine, mine, 0)
    index = jnp.arange(mine, dtype=jnp.int32)
    ahead = (lens[None, :] > lens[:, None]) | ((lens[None, :] == lens[:, None]) & (index[None, :] < index[:, None]))
    rank = jnp.sum(ahead.astype(jnp.int32), axis=1)
    at = rank[None, :] == index[:, None]
    order = jnp.sum(jnp.where(at, index[None, :], 0), axis=1)
    sorted_lens = jnp.sum(jnp.where(at, lens[None, :], 0), axis=1)
    wide_lens = jnp.broadcast_to(sorted_lens[:, None], (mine, LANES))
    row = jnp.arange(LANES)
    same = row[:, None] // mine == row[None, :] // mine
    sort = (same & (jnp.tile(rank, LANES // mine)[None, :] == row[:, None] % mine)).astype(bf16)
    tall = jnp.broadcast_to(jnp.tile(lens, LANES // mine)[:, None], (LANES, LANES))
    slab, chunk = jnp.array(SLABS)[:, None], jnp.arange(chunks)[None, :]
    least = ((tok ^ slab) * slots + chunk * CHUNK).reshape(-1)
    used = jnp.sum((sorted_lens[::GROUP][None, :] > least[:, None]).astype(jnp.int32), axis=1)
    entry = jnp.arange(tok_size * chunks + 1)
    starts = jnp.sum(jnp.where(entry[None, :-1] < entry[:, None], used[None, :], 0), axis=1)

    def packed_shape(lists):
        return jax.ShapeDtypeStruct(((lists * chunks + 1) * groups * BLOCK, width), bf16)

    def tops(lists, steps=1):
        return pltpu.VMEM(((lists * chunks + 1) * groups * GROUP, steps * columns), f32)

    shapes = dict(slots=slots, chunks=chunks)
    best_shape = jax.ShapeDtypeStruct((mine, columns), f32)
    near_packed = call(
        functools.partial(pack_kernel, **shapes), "pack_near", packed_shape(2), [], (starts,), sort, tall, own, near,
    )
    pair = (arrived, swapped(arrived, 1))
    best = call(
        functools.partial(early_kernel, **shapes), "early", best_shape, [tops(2)], (starts,),
        wide_lens, near_packed, *pair,
    )
    relayed, best = lax.optimization_barrier((relayed, best))
    last_pair = (relayed, swapped(relayed, 1))
    far_packed, best = call(
        functools.partial(middle_kernel, **shapes), "middle", (packed_shape(1), best_shape), [tops(1)], (starts,),
        wide_lens, sort, tall, fars[0], *pair, best,
    )
    second = call(
        functools.partial(second_kernel, **shapes), "second", best_shape, [tops(2), tops(1)], (starts,),
        wide_lens, near_packed, far_packed, *last_pair,
    )
    scores = call(
        functools.partial(late_kernel, **shapes), "late", jax.ShapeDtypeStruct((mine, LANES), f32),
        [
            pltpu.VMEM((mine, columns), f32),
            pltpu.VMEM(packed_shape(1).shape, bf16),
            tops(1, STEPS),
            pltpu.VMEM((mine, LANES), f32),
        ],
        (starts, order), wide_lens, sort, tall, fars[1], *pair, *last_pair, best, second,
    )

    chip = in_order(scores, swapped(scores, 1), core == 0)
    sent = jnp.where(core == 0, chip[:, :qcount], chip[:, qcount:])
    block = in_order(returned(sent, 0), returned(sent, 2), tok < 2)
    both = in_order(block[None], swapped(block, 1)[None], core == 0)
    return jnp.transpose(both, (2, 0, 1))


def solution(mesh):
    in_specs = (P("dp", None, None), P("dp", "tok", None), P())
    out_specs = P("dp", None, None)
    return jax.shard_map(per_device, mesh=mesh, in_specs=in_specs, out_specs=out_specs, check_vma=False)
```

```python
import functools

import jax
import jax.numpy as jnp
from jax import lax
from jax.experimental import pallas as pl
from jax.experimental.pallas import tpu as pltpu
from jax.sharding import PartitionSpec as P

STEPS = 2
NEGATIVE_FILL = -1e30
CHUNK = 16
GROUP = 8
BLOCK = CHUNK * GROUP
BATCH = 8
COLUMNS = 256
LANES = 128
RUN = 8
FAR = (3, 2)
SLABS = (0, 1) + FAR
VMEM_LIMIT = 40 * 1024 * 1024
CUT_VMEM_LIMIT = 62 * 1024 * 1024
SMEM = pl.BlockSpec(memory_space=pltpu.SMEM)
VMEM = pl.BlockSpec(memory_space=pltpu.VMEM)
HBM = pl.BlockSpec(memory_space=pltpu.HBM)


def normalized(values):
    wide = values.astype(jnp.float32)
    return wide * lax.rsqrt(jnp.sum(wide * wide, axis=-1, keepdims=True) + 1e-06)


def prepare_kernel(half_ref, out_ref, wide_ref):
    count, tokens, _ = half_ref.shape

    def norm_one(i, carry):
        rows = pl.ds(pl.multiple_of(i * tokens, tokens), tokens)
        wide_ref[rows, :] = normalized(half_ref[i])
        return carry

    lax.fori_loop(0, count, norm_one, 0, unroll=16)

    def place_token(k, carry):
        out_ref[k] = wide_ref[pl.ds(k, count, stride=tokens), :].astype(out_ref.dtype)
        return carry

    lax.fori_loop(0, tokens, place_token, 0, unroll=16)


def cut_kernel(docs_ref, after_ref, *refs):
    del after_ref
    *slab_refs, sems = refs
    mine = slab_refs[0].shape[1]
    cuts = []
    for n in (2, 3, 1, 0):
        first = pl.multiple_of((lax.axis_index("tok") ^ SLABS[n]) * mine, mine)
        cuts.append(pltpu.make_async_copy(docs_ref.at[:, pl.ds(first, mine), :], slab_refs[n], sems.at[n]))
        cuts[-1].start()
    for cut in cuts:
        cut.wait()


def pack(slab_ref, base, starts, first_entry, offset, sort_ref, tall_ref, packed_ref):
    slots, docs, width = slab_ref.shape
    groups = docs // GROUP
    step = sort_ref.shape[0] // docs
    first = normalized(slab_ref[0])
    firsts = jnp.concatenate([first] * step, axis=0)
    slot = lax.broadcasted_iota(jnp.int32, (step * docs, 1), 0) // docs + base
    for u in range(0, -(-slots // CHUNK) * CHUNK, step):
        inside = min(slots - u, step)
        rows = normalized(slab_ref[u : u + inside]).reshape(inside * docs, width)
        if inside < step:
            rows = jnp.concatenate([rows] + [first] * (step - inside), axis=0)
        rows = jnp.where(slot + u < tall_ref[...], rows, firsts).astype(packed_ref.dtype)
        rows = jnp.dot(sort_ref[...], rows, preferred_element_type=jnp.float32)
        start = (starts[first_entry + u // CHUNK] - offset) * BLOCK
        for g in range(groups):
            for v in range(0, step, 2):
                both = [rows[(v + e) * docs + g * GROUP : (v + e) * docs + (g + 1) * GROUP] for e in range(2)]
                at = pl.multiple_of(start + (g * BLOCK + (u % CHUNK + v) * GROUP), 2 * GROUP)
                packed_ref[pl.ds(at, 2 * GROUP), :] = jnp.concatenate(both, axis=0).astype(packed_ref.dtype)


def multiply(packed_ref, count, q_refs, top_ref, batch_blocks=BATCH):
    tokens, queries, width = q_refs[0].shape
    step = COLUMNS // queries

    def run(s, blocks):
        rows = packed_ref[pl.ds(pl.multiple_of(s * BLOCK, BLOCK), blocks * BLOCK), :]
        at = 0
        for q_ref in q_refs:
            for k in range(0, tokens, step):
                q = q_ref[k : k + step].reshape(COLUMNS, width)
                similar = lax.dot_general(rows, q, (((1,), (1,)), ((), ())), preferred_element_type=jnp.float32)
                top = jnp.max(similar.reshape(blocks, CHUNK, GROUP, COLUMNS), axis=1)
                place = pl.ds(pl.multiple_of(s * GROUP, GROUP), blocks * GROUP)
                top_ref[place, at : at + COLUMNS] = top.reshape(blocks * GROUP, COLUMNS)
                at += COLUMNS

    def batch(i, carry):
        run(i * batch_blocks, batch_blocks)
        return carry

    lax.fori_loop(0, count // batch_blocks, batch, 0)
    size = batch_blocks // 2
    while size:
        done = count // (2 * size) * (2 * size)

        @pl.when(count - done >= size)
        def _(size=size, done=done):
            run(done, size)

        size //= 2


def combine(top_ref, lists, offset, starts, lens_ref, old_ref, best_ref, slots, first=0):
    docs, columns = best_ref.shape
    chunks = (starts.shape[0] - 1) // 4
    for g in range(docs // GROUP):
        rows = slice(g * GROUP, (g + 1) * GROUP)
        lens = lens_ref[rows, 0:1]
        best = jnp.full((GROUP, columns), NEGATIVE_FILL, jnp.float32) if old_ref is None else old_ref[rows, :]
        for which in lists:
            for c in range(chunks):
                at = pl.multiple_of((starts[which * chunks + c] - offset + g) * GROUP, GROUP)
                top = top_ref[pl.ds(at, GROUP), first : first + columns]
                real = lens > (lax.axis_index("tok") ^ SLABS[which]) * slots + c * CHUNK
                best = jnp.maximum(best, jnp.where(real, top, NEGATIVE_FILL))
        best_ref[rows, :] = best


def pack_kernel(starts, sort, tall, own, near, packed_ref, *, slots, chunks):
    tok = lax.axis_index("tok")
    for k, slab in enumerate((own, near)):
        pack(slab, (tok ^ k) * slots, starts, k * chunks, 0, sort, tall, packed_ref)


def early_kernel(starts, lens, packed, qa, qb, best_ref, top_ref, *, slots, chunks):
    multiply(packed, starts[2 * chunks], (qa, qb), top_ref)
    combine(top_ref, (0, 1), 0, starts, lens, None, best_ref, slots)


def middle_kernel(starts, lens, sort, tall, far, qa, qb, old, packed_ref, best_ref, top_ref, *, slots, chunks):
    offset = starts[2 * chunks]
    pack(far, (lax.axis_index("tok") ^ FAR[0]) * slots, starts, 2 * chunks, offset, sort, tall, packed_ref)
    multiply(packed_ref, starts[3 * chunks] - offset, (qa, qb), top_ref)
    combine(top_ref, (2,), offset, starts, lens, old, best_ref, slots)


def second_kernel(starts, lens, near_packed, far_packed, qa, qb, best_ref, near_top, far_top, *, slots, chunks):
    offset = starts[2 * chunks]
    multiply(near_packed, offset, (qa, qb), near_top)
    multiply(far_packed, starts[3 * chunks] - offset, (qa, qb), far_top)
    combine(near_top, (0, 1), 0, starts, lens, None, best_ref, slots)
    combine(far_top, (2,), offset, starts, lens, best_ref, best_ref, slots)


def query_sums(best_ref, step_no, tok, count):
    docs, columns = best_ref.shape
    half = lax.rem(tok, 2)
    lane_group = lax.broadcasted_iota(jnp.int32, (docs, LANES), 1) // count
    merged = jnp.zeros((docs, LANES), jnp.float32)
    for other in range(2):
        at = other * columns // 2
        total = best_ref[:, at : at + LANES]
        for k in range(at + LANES, at + columns // 2, LANES):
            total = total + best_ref[:, k : k + LANES]
        shift = LANES // 2
        while shift >= count:
            total = total + pltpu.roll(total, shift, 1)
            shift //= 2
        place = 2 * step_no + (half if other == 0 else 1 - half)
        merged = jnp.where(lane_group == place, total, merged)
    return merged


def late_kernel(
    starts, order, lens, sort, tall, far, q1a, q1b, q2a, q2b, old1, old2, out_ref,
    best_ref, packed_ref, top_ref, sums_ref, *, slots, chunks,
):
    tok = lax.axis_index("tok")
    offset = starts[3 * chunks]
    pack(far, (tok ^ FAR[1]) * slots, starts, 3 * chunks, offset, sort, tall, packed_ref)
    multiply(packed_ref, starts[4 * chunks] - offset, (q1a, q1b, q2a, q2b), top_ref, BATCH // 2)
    docs, columns = best_ref.shape
    total = jnp.zeros((docs, LANES), jnp.float32)
    for s, old in enumerate((old1, old2)):
        combine(top_ref, (3,), offset, starts, lens, old, best_ref, slots, s * columns)
        total = total + query_sums(best_ref, s, tok, q1a.shape[1])
    sums_ref[...] = total

    def unsort(p, carry):
        out_ref[pl.ds(order[p], 1), :] = sums_ref[pl.ds(p, 1), :]
        return carry

    lax.fori_loop(0, docs, unsort, 0, unroll=8)


def handed_back(block, shift, chosen=lambda dp: True):
    dp_size, tok_size = lax.axis_size("dp"), lax.axis_size("tok")
    route = []
    for i in filter(chosen, range(dp_size)):
        for t in range(tok_size):
            mask = 2 if t % 2 and i % (dp_size // 2) < shift else 0
            route.append((i * tok_size + t, (i - shift) % dp_size * tok_size + (t ^ mask)))
    return lax.ppermute(block, ("dp", "tok"), route)


def swapped(block, mask):
    return lax.ppermute(block, "tok", [(i, i ^ mask) for i in range(lax.axis_size("tok"))])


def returned(block, mask):
    dp_size, tok_size = lax.axis_size("dp"), lax.axis_size("tok")
    route = [
        (i * tok_size + t, (i + 1 + t % 2) % dp_size * tok_size + (t ^ mask))
        for i in range(dp_size)
        for t in range(tok_size)
    ]
    return lax.ppermute(block, ("dp", "tok"), route)


def in_order(own, other, own_first):
    return jnp.where(own_first, jnp.concatenate([own, other], axis=0), jnp.concatenate([other, own], axis=0))


def per_device(queries, documents, lengths):
    qcount, tokens, width = queries.shape
    dcount, slots, _ = documents.shape
    tok_size = lax.axis_size("tok")
    tok, dp = lax.axis_index("tok"), lax.axis_index("dp")
    core = tok % 2
    mine = dcount // tok_size
    half = qcount // 2
    columns = qcount * tokens
    chunks = -(-slots // CHUNK)
    groups = mine // GROUP
    params = pltpu.CompilerParams(vmem_limit_bytes=VMEM_LIMIT)
    cost = pl.CostEstimate(flops=1 << 10, bytes_accessed=1 << 10, transcendentals=0)
    bf16, f32 = jnp.bfloat16, jnp.float32

    def call(kernel, name, out_shape, scratch_shapes, scalars, *operands):
        return pl.pallas_call(
            kernel,
            out_shape=out_shape,
            in_specs=[SMEM] * len(scalars) + [VMEM] * len(operands),
            out_specs=jax.tree.map(lambda _: VMEM, out_shape),
            scratch_shapes=scratch_shapes,
            compiler_params=params,
            cost_estimate=cost,
            name=name,
        )(*scalars, *operands)

    prepared = call(
        prepare_kernel, "prepare", jax.ShapeDtypeStruct((tokens, half, width), bf16),
        [pltpu.VMEM((half * tokens, width), f32)], (), lax.dynamic_slice_in_dim(queries, core * half, half, 0),
    )
    arrived = handed_back(prepared, 1)
    slabs = pl.pallas_call(
        cut_kernel,
        out_shape=(jax.ShapeDtypeStruct((slots, mine, width), bf16),) * tok_size,
        in_specs=[HBM, HBM],
        out_specs=(VMEM,) * tok_size,
        scratch_shapes=[pltpu.SemaphoreType.DMA((tok_size,))],
        compiler_params=pltpu.CompilerParams(vmem_limit_bytes=CUT_VMEM_LIMIT),
        cost_estimate=cost,
        name="cut",
    )(jnp.transpose(documents, (1, 0, 2)), prepared)
    own, prepared = lax.optimization_barrier((slabs[0], prepared))
    relayed = handed_back(arrived, 1, lambda i: i % RUN != 0) + handed_back(prepared, 2, lambda i: i % RUN == 1)
    near, *fars = [swapped(slabs[n], SLABS[n]) for n in (1, 2, 3)]

    lens = lax.dynamic_slice_in_dim(lengths, dp * dcount + tok * mine, mine, 0)
    index = jnp.arange(mine, dtype=jnp.int32)
    ahead = (lens[None, :] > lens[:, None]) | ((lens[None, :] == lens[:, None]) & (index[None, :] < index[:, None]))
    rank = jnp.sum(ahead.astype(jnp.int32), axis=1)
    at = rank[None, :] == index[:, None]
    order = jnp.sum(jnp.where(at, index[None, :], 0), axis=1)
    sorted_lens = jnp.sum(jnp.where(at, lens[None, :], 0), axis=1)
    wide_lens = jnp.broadcast_to(sorted_lens[:, None], (mine, LANES))
    row = jnp.arange(LANES)
    same = row[:, None] // mine == row[None, :] // mine
    sort = (same & (jnp.tile(rank, LANES // mine)[None, :] == row[:, None] % mine)).astype(bf16)
    tall = jnp.broadcast_to(jnp.tile(lens, LANES // mine)[:, None], (LANES, LANES))
    slab, chunk = jnp.array(SLABS)[:, None], jnp.arange(chunks)[None, :]
    least = ((tok ^ slab) * slots + chunk * CHUNK).reshape(-1)
    used = jnp.sum((sorted_lens[::GROUP][None, :] > least[:, None]).astype(jnp.int32), axis=1)
    entry = jnp.arange(tok_size * chunks + 1)
    starts = jnp.sum(jnp.where(entry[None, :-1] < entry[:, None], used[None, :], 0), axis=1)

    def packed_shape(lists):
        return jax.ShapeDtypeStruct(((lists * chunks + 1) * groups * BLOCK, width), bf16)

    def tops(lists, steps=1):
        return pltpu.VMEM(((lists * chunks + 1) * groups * GROUP, steps * columns), f32)

    shapes = dict(slots=slots, chunks=chunks)
    best_shape = jax.ShapeDtypeStruct((mine, columns), f32)
    near_packed = call(
        functools.partial(pack_kernel, **shapes), "pack_near", packed_shape(2), [], (starts,), sort, tall, own, near,
    )
    pair = (arrived, swapped(arrived, 1))
    best = call(
        functools.partial(early_kernel, **shapes), "early", best_shape, [tops(2)], (starts,),
        wide_lens, near_packed, *pair,
    )
    far_packed, best = call(
        functools.partial(middle_kernel, **shapes), "middle", (packed_shape(1), best_shape), [tops(1)], (starts,),
        wide_lens, sort, tall, fars[0], *pair, best,
    )
    relayed, best = lax.optimization_barrier((relayed, best))
    last_pair = (relayed, swapped(relayed, 1))
    second = call(
        functools.partial(second_kernel, **shapes), "second", best_shape, [tops(2), tops(1)], (starts,),
        wide_lens, near_packed, far_packed, *last_pair,
    )
    scores = call(
        functools.partial(late_kernel, **shapes), "late", jax.ShapeDtypeStruct((mine, LANES), f32),
        [
            pltpu.VMEM((mine, columns), f32),
            pltpu.VMEM(packed_shape(1).shape, bf16),
            tops(1, STEPS),
            pltpu.VMEM((mine, LANES), f32),
        ],
        (starts, order), wide_lens, sort, tall, fars[1], *pair, *last_pair, best, second,
    )

    chip = in_order(scores, swapped(scores, 1), core == 0)
    sent = jnp.where(core == 0, chip[:, :qcount], chip[:, qcount:])
    block = in_order(returned(sent, 0), returned(sent, 2), tok < 2)
    both = in_order(block[None], swapped(block, 1)[None], core == 0)
    return jnp.transpose(both, (2, 0, 1))


def solution(mesh):
    in_specs = (P("dp", None, None), P("dp", "tok", None), P())
    out_specs = P("dp", None, None)
    return jax.shard_map(per_device, mesh=mesh, in_specs=in_specs, out_specs=out_specs, check_vma=False)
```

```python
import functools

import jax
import jax.numpy as jnp
from jax import lax
from jax.experimental import pallas as pl
from jax.experimental.pallas import tpu as pltpu
from jax.sharding import PartitionSpec as P

STEPS = 2
NEGATIVE_FILL = -1e30
CHUNK = 16
GROUP = 8
BLOCK = CHUNK * GROUP
BATCH = 8
COLUMNS = 256
LANES = 128
RUN = 8
FAR = (3, 2)
SLABS = (0, 1) + FAR
VMEM_LIMIT = 40 * 1024 * 1024
CUT_VMEM_LIMIT = 62 * 1024 * 1024
SMEM = pl.BlockSpec(memory_space=pltpu.SMEM)
VMEM = pl.BlockSpec(memory_space=pltpu.VMEM)
HBM = pl.BlockSpec(memory_space=pltpu.HBM)


def normalized(values):
    wide = values.astype(jnp.float32)
    return wide * lax.rsqrt(jnp.sum(wide * wide, axis=-1, keepdims=True) + 1e-06)


def prepare_kernel(half_ref, out_ref, wide_ref):
    count, tokens, _ = half_ref.shape

    def norm_one(i, carry):
        rows = pl.ds(pl.multiple_of(i * tokens, tokens), tokens)
        wide_ref[rows, :] = normalized(half_ref[i])
        return carry

    lax.fori_loop(0, count, norm_one, 0, unroll=16)

    def place_token(k, carry):
        out_ref[k] = wide_ref[pl.ds(k, count, stride=tokens), :].astype(out_ref.dtype)
        return carry

    lax.fori_loop(0, tokens, place_token, 0, unroll=16)


def cut_kernel(docs_ref, after_ref, *refs):
    del after_ref
    *slab_refs, sems = refs
    mine = slab_refs[0].shape[1]
    cuts = []
    for n in (2, 3, 1):
        first = pl.multiple_of((lax.axis_index("tok") ^ SLABS[n]) * mine, mine)
        cuts.append(pltpu.make_async_copy(docs_ref.at[:, pl.ds(first, mine), :], slab_refs[n - 1], sems.at[n]))
        cuts[-1].start()
    for cut in cuts:
        cut.wait()


def pack(slab_ref, base, starts, first_entry, offset, sort_ref, tall_ref, packed_ref):
    slots, docs, width = slab_ref.shape
    groups = docs // GROUP
    step = sort_ref.shape[0] // docs
    first = normalized(slab_ref[0])
    firsts = jnp.concatenate([first] * step, axis=0)
    slot = lax.broadcasted_iota(jnp.int32, (step * docs, 1), 0) // docs + base
    for u in range(0, -(-slots // CHUNK) * CHUNK, step):
        inside = min(slots - u, step)
        rows = normalized(slab_ref[u : u + inside]).reshape(inside * docs, width)
        if inside < step:
            rows = jnp.concatenate([rows] + [first] * (step - inside), axis=0)
        rows = jnp.where(slot + u < tall_ref[...], rows, firsts).astype(packed_ref.dtype)
        rows = jnp.dot(sort_ref[...], rows, preferred_element_type=jnp.float32)
        start = (starts[first_entry + u // CHUNK] - offset) * BLOCK
        for g in range(groups):
            for v in range(0, step, 2):
                both = [rows[(v + e) * docs + g * GROUP : (v + e) * docs + (g + 1) * GROUP] for e in range(2)]
                at = pl.multiple_of(start + (g * BLOCK + (u % CHUNK + v) * GROUP), 2 * GROUP)
                packed_ref[pl.ds(at, 2 * GROUP), :] = jnp.concatenate(both, axis=0).astype(packed_ref.dtype)


def multiply(packed_ref, count, q_refs, top_ref, batch_blocks=BATCH):
    tokens, queries, width = q_refs[0].shape
    step = COLUMNS // queries

    def run(s, blocks):
        rows = packed_ref[pl.ds(pl.multiple_of(s * BLOCK, BLOCK), blocks * BLOCK), :]
        at = 0
        for q_ref in q_refs:
            for k in range(0, tokens, step):
                q = q_ref[k : k + step].reshape(COLUMNS, width)
                similar = lax.dot_general(rows, q, (((1,), (1,)), ((), ())), preferred_element_type=jnp.float32)
                top = jnp.max(similar.reshape(blocks, CHUNK, GROUP, COLUMNS), axis=1)
                place = pl.ds(pl.multiple_of(s * GROUP, GROUP), blocks * GROUP)
                top_ref[place, at : at + COLUMNS] = top.reshape(blocks * GROUP, COLUMNS)
                at += COLUMNS

    def batch(i, carry):
        run(i * batch_blocks, batch_blocks)
        return carry

    lax.fori_loop(0, count // batch_blocks, batch, 0)
    size = batch_blocks // 2
    while size:
        done = count // (2 * size) * (2 * size)

        @pl.when(count - done >= size)
        def _(size=size, done=done):
            run(done, size)

        size //= 2


def combine(top_ref, lists, offset, starts, lens_ref, old_ref, best_ref, slots, first=0):
    docs, columns = best_ref.shape
    chunks = (starts.shape[0] - 1) // 4
    for g in range(docs // GROUP):
        rows = slice(g * GROUP, (g + 1) * GROUP)
        lens = lens_ref[rows, 0:1]
        best = jnp.full((GROUP, columns), NEGATIVE_FILL, jnp.float32) if old_ref is None else old_ref[rows, :]
        for which in lists:
            for c in range(chunks):
                at = pl.multiple_of((starts[which * chunks + c] - offset + g) * GROUP, GROUP)
                top = top_ref[pl.ds(at, GROUP), first : first + columns]
                real = lens > (lax.axis_index("tok") ^ SLABS[which]) * slots + c * CHUNK
                best = jnp.maximum(best, jnp.where(real, top, NEGATIVE_FILL))
        best_ref[rows, :] = best


def pack_kernel(starts, sort, tall, own, near, packed_ref, *, slots, chunks):
    tok = lax.axis_index("tok")
    for k, slab in enumerate((own, near)):
        pack(slab, (tok ^ k) * slots, starts, k * chunks, 0, sort, tall, packed_ref)


def early_kernel(starts, lens, packed, qa, qb, best_ref, top_ref, *, slots, chunks):
    multiply(packed, starts[2 * chunks], (qa, qb), top_ref)
    combine(top_ref, (0, 1), 0, starts, lens, None, best_ref, slots)


def middle_kernel(starts, lens, sort, tall, far, qa, qb, old, packed_ref, best_ref, top_ref, *, slots, chunks):
    offset = starts[2 * chunks]
    pack(far, (lax.axis_index("tok") ^ FAR[0]) * slots, starts, 2 * chunks, offset, sort, tall, packed_ref)
    multiply(packed_ref, starts[3 * chunks] - offset, (qa, qb), top_ref)
    combine(top_ref, (2,), offset, starts, lens, old, best_ref, slots)


def second_kernel(starts, lens, near_packed, far_packed, qa, qb, best_ref, near_top, far_top, *, slots, chunks):
    offset = starts[2 * chunks]
    multiply(near_packed, offset, (qa, qb), near_top)
    multiply(far_packed, starts[3 * chunks] - offset, (qa, qb), far_top)
    combine(near_top, (0, 1), 0, starts, lens, None, best_ref, slots)
    combine(far_top, (2,), offset, starts, lens, best_ref, best_ref, slots)


def query_sums(best_ref, step_no, tok, count):
    docs, columns = best_ref.shape
    half = lax.rem(tok, 2)
    lane_group = lax.broadcasted_iota(jnp.int32, (docs, LANES), 1) // count
    merged = jnp.zeros((docs, LANES), jnp.float32)
    for other in range(2):
        at = other * columns // 2
        total = best_ref[:, at : at + LANES]
        for k in range(at + LANES, at + columns // 2, LANES):
            total = total + best_ref[:, k : k + LANES]
        shift = LANES // 2
        while shift >= count:
            total = total + pltpu.roll(total, shift, 1)
            shift //= 2
        place = 2 * step_no + (half if other == 0 else 1 - half)
        merged = jnp.where(lane_group == place, total, merged)
    return merged


def late_kernel(
    starts, order, lens, sort, tall, far, q1a, q1b, q2a, q2b, old1, old2, out_ref,
    best_ref, packed_ref, top_ref, sums_ref, *, slots, chunks,
):
    tok = lax.axis_index("tok")
    offset = starts[3 * chunks]
    pack(far, (tok ^ FAR[1]) * slots, starts, 3 * chunks, offset, sort, tall, packed_ref)
    multiply(packed_ref, starts[4 * chunks] - offset, (q1a, q1b, q2a, q2b), top_ref, BATCH // 2)
    docs, columns = best_ref.shape
    total = jnp.zeros((docs, LANES), jnp.float32)
    for s, old in enumerate((old1, old2)):
        combine(top_ref, (3,), offset, starts, lens, old, best_ref, slots, s * columns)
        total = total + query_sums(best_ref, s, tok, q1a.shape[1])
    sums_ref[...] = total

    def unsort(p, carry):
        out_ref[pl.ds(order[p], 1), :] = sums_ref[pl.ds(p, 1), :]
        return carry

    lax.fori_loop(0, docs, unsort, 0, unroll=8)


def wraps(dp, shift):
    return dp % RUN < shift


def handed_back(block, shift, chosen=lambda dp: True):
    dp_size, tok_size = lax.axis_size("dp"), lax.axis_size("tok")
    route = []
    for i in filter(chosen, range(dp_size)):
        for t in range(tok_size):
            mask = 2 if t % 2 and i % (dp_size // 2) < shift else 0
            route.append((i * tok_size + t, (i - shift) % dp_size * tok_size + (t ^ mask)))
    return lax.ppermute(block, ("dp", "tok"), route)


def swapped(block, mask):
    return lax.ppermute(block, "tok", [(i, i ^ mask) for i in range(lax.axis_size("tok"))])


def returned(block, mask):
    dp_size, tok_size = lax.axis_size("dp"), lax.axis_size("tok")
    route = [
        (i * tok_size + t, (i + 1 + t % 2) % dp_size * tok_size + (t ^ mask))
        for i in range(dp_size)
        for t in range(tok_size)
    ]
    return lax.ppermute(block, ("dp", "tok"), route)


def in_order(own, other, own_first):
    return jnp.where(own_first, jnp.concatenate([own, other], axis=0), jnp.concatenate([other, own], axis=0))


def per_device(queries, documents, lengths):
    qcount, tokens, width = queries.shape
    dcount, slots, _ = documents.shape
    tok_size = lax.axis_size("tok")
    tok, dp = lax.axis_index("tok"), lax.axis_index("dp")
    core = tok % 2
    mine = dcount // tok_size
    half = qcount // 2
    columns = qcount * tokens
    chunks = -(-slots // CHUNK)
    groups = mine // GROUP
    params = pltpu.CompilerParams(vmem_limit_bytes=VMEM_LIMIT)
    cost = pl.CostEstimate(flops=1 << 10, bytes_accessed=1 << 10, transcendentals=0)
    bf16, f32 = jnp.bfloat16, jnp.float32

    def call(kernel, name, out_shape, scratch_shapes, scalars, *operands):
        return pl.pallas_call(
            kernel,
            out_shape=out_shape,
            in_specs=[SMEM] * len(scalars) + [VMEM] * len(operands),
            out_specs=jax.tree.map(lambda _: VMEM, out_shape),
            scratch_shapes=scratch_shapes,
            compiler_params=params,
            cost_estimate=cost,
            name=name,
        )(*scalars, *operands)

    prepared = call(
        prepare_kernel, "prepare", jax.ShapeDtypeStruct((tokens, half, width), bf16),
        [pltpu.VMEM((half * tokens, width), f32)], (), lax.dynamic_slice_in_dim(queries, core * half, half, 0),
    )
    arrived = handed_back(prepared, 1)
    by_slot = jnp.transpose(documents, (1, 0, 2))
    cut = pl.pallas_call(
        cut_kernel,
        out_shape=(jax.ShapeDtypeStruct((slots, mine, width), bf16),) * (tok_size - 1),
        in_specs=[HBM, HBM],
        out_specs=(VMEM,) * (tok_size - 1),
        scratch_shapes=[pltpu.SemaphoreType.DMA((tok_size,))],
        compiler_params=pltpu.CompilerParams(vmem_limit_bytes=CUT_VMEM_LIMIT),
        cost_estimate=cost,
        name="cut",
    )(by_slot, prepared)
    slabs = [None, *cut]
    sent_slab, prepared = lax.optimization_barrier((cut[0], prepared))
    slabs[1] = sent_slab
    own = lax.dynamic_slice_in_dim(by_slot, tok * mine, mine, 1)
    relayed = handed_back(arrived, 1, lambda i: not wraps(i + 1, 2)) + handed_back(prepared, 2, lambda i: wraps(i, 2))
    near, *fars = [swapped(slabs[n], SLABS[n]) for n in (1, 2, 3)]

    lens = lax.dynamic_slice_in_dim(lengths, dp * dcount + tok * mine, mine, 0)
    lens, own = lax.optimization_barrier((lens, own))
    index = jnp.arange(mine, dtype=jnp.int32)
    ahead = (lens[None, :] > lens[:, None]) | ((lens[None, :] == lens[:, None]) & (index[None, :] < index[:, None]))
    rank = jnp.sum(ahead.astype(jnp.int32), axis=1)
    at = rank[None, :] == index[:, None]
    order = jnp.sum(jnp.where(at, index[None, :], 0), axis=1)
    sorted_lens = jnp.sum(jnp.where(at, lens[None, :], 0), axis=1)
    wide_lens = jnp.broadcast_to(sorted_lens[:, None], (mine, LANES))
    row = jnp.arange(LANES)
    same = row[:, None] // mine == row[None, :] // mine
    sort = (same & (jnp.tile(rank, LANES // mine)[None, :] == row[:, None] % mine)).astype(bf16)
    tall = jnp.broadcast_to(jnp.tile(lens, LANES // mine)[:, None], (LANES, LANES))
    slab, chunk = jnp.array(SLABS)[:, None], jnp.arange(chunks)[None, :]
    least = ((tok ^ slab) * slots + chunk * CHUNK).reshape(-1)
    used = jnp.sum((sorted_lens[::GROUP][None, :] > least[:, None]).astype(jnp.int32), axis=1)
    entry = jnp.arange(tok_size * chunks + 1)
    starts = jnp.sum(jnp.where(entry[None, :-1] < entry[:, None], used[None, :], 0), axis=1)

    def packed_shape(lists):
        return jax.ShapeDtypeStruct(((lists * chunks + 1) * groups * BLOCK, width), bf16)

    def tops(lists, steps=1):
        return pltpu.VMEM(((lists * chunks + 1) * groups * GROUP, steps * columns), f32)

    shapes = dict(slots=slots, chunks=chunks)
    best_shape = jax.ShapeDtypeStruct((mine, columns), f32)
    near_packed = call(
        functools.partial(pack_kernel, **shapes), "pack_near", packed_shape(2), [], (starts,), sort, tall, own, near,
    )
    pair = (arrived, swapped(arrived, 1))
    best = call(
        functools.partial(early_kernel, **shapes), "early", best_shape, [tops(2)], (starts,),
        wide_lens, near_packed, *pair,
    )
    relayed, best = lax.optimization_barrier((relayed, best))
    last_pair = (relayed, swapped(relayed, 1))
    far_packed, best = call(
        functools.partial(middle_kernel, **shapes), "middle", (packed_shape(1), best_shape), [tops(1)], (starts,),
        wide_lens, sort, tall, fars[0], *pair, best,
    )
    second = call(
        functools.partial(second_kernel, **shapes), "second", best_shape, [tops(2), tops(1)], (starts,),
        wide_lens, near_packed, far_packed, *last_pair,
    )
    scores = call(
        functools.partial(late_kernel, **shapes), "late", jax.ShapeDtypeStruct((mine, LANES), f32),
        [
            pltpu.VMEM((mine, columns), f32),
            pltpu.VMEM(packed_shape(1).shape, bf16),
            tops(1, STEPS),
            pltpu.VMEM((mine, LANES), f32),
        ],
        (starts, order), wide_lens, sort, tall, fars[1], *pair, *last_pair, best, second,
    )

    chip = in_order(scores, swapped(scores, 1), core == 0)
    sent = jnp.where(core == 0, chip[:, :qcount], chip[:, qcount:])
    block = in_order(returned(sent, 0), returned(sent, 2), tok < 2)
    both = in_order(block[None], swapped(block, 1)[None], core == 0)
    return jnp.transpose(both, (2, 0, 1))


def solution(mesh):
    in_specs = (P("dp", None, None), P("dp", "tok", None), P())
    out_specs = P("dp", None, None)
    return jax.shard_map(per_device, mesh=mesh, in_specs=in_specs, out_specs=out_specs, check_vma=False)
```
